32 devices in a mesh: dp: 4 (over x, core), ctx: 8 (over z, y).
Axes of the slice: x: 2, y: 2, z: 4, core: 2. Of those that a mesh axis runs over, the one named last changes fastest.
Arguments:
- qkv: bfloat16 [4, 3, 4096, 1024], P('dp', None, None, 'ctx'), may hold values from -6 to 6
- taps: float32 [3, 3, 4096], P(None, None, 'ctx'), may hold values from -3.5 to 3.5
- rate_table: float32 [16, 4096], P('dp', 'ctx'), may hold values from 0.00029296875 to 2, as said below
- residue_table: float32 [16, 4096], P('dp', 'ctx'), may hold values from -5 to 5
- bias: float32 [4096], P('ctx'), may hold values from -0.5 to 0.5
Outputs:
- mixed: bfloat16 [4, 4096, 1024], P('dp', None, 'ctx')
The draws below stay inside these ranges and needn't reach their ends.
Inputs may be any that keep to these rules, and one draw needn't show every extreme that they name: `rate_table`: every rate is positive.
All inputs are finite; a program needn't handle non-finite values.
Results may differ from the reference program's by a relative error of at most 0.0085.
Values may be sent and summed in bfloat16 or wider, within the bound.
A program may use at most 320 MiB of HBM per device.

```python
import math
import jax
import jax.numpy as jnp
from jax import lax

C = 4096
ORDER = 16
STREAMS = 4
LENGTH = 1024


def draw_rate_table(key, part):
    key = jax.random.fold_in(key, 7)
    wide_key = jax.random.fold_in(key, 1)
    lowest = math.log(0.3 / LENGTH)
    highest = math.log(2.0)
    wide = jnp.exp(jax.random.uniform(wide_key, (ORDER, C), jnp.float32, lowest, highest))
    rates = wide
    return jnp.clip(rates, 0.3 / LENGTH, 2.0).astype(jnp.float32)


def draw_residue_table(key, part):
    key = jax.random.fold_in(key, 11)
    base_key, pick_key, size_key, sign_key = jax.random.split(key, 4)
    leader = jax.random.randint(pick_key, (C,), 0, ORDER)
    marked = jnp.arange(ORDER)[:, None] == leader[None, :]
    signs = (2 * jax.random.randint(sign_key, (C,), 0, 2) - 1).astype(jnp.float32)
    base = jnp.clip(0.4 * jax.random.normal(base_key, (ORDER, C), jnp.float32), -2.0, 2.0)
    magnitude = jax.random.uniform(size_key, (C,), jnp.float32, 4.0, 5.0)
    return jnp.where(marked, (signs * magnitude)[None, :], base).astype(jnp.float32)


def level_of(own_key, shape, cuts, low, high):
    gain = 1.0
    for position, shards_of in cuts:
        draws = jax.random.uniform(jax.random.fold_in(jax.random.fold_in(own_key, 6), position), (shards_of,), jnp.float32, low / len(cuts), high / len(cuts))
        gain = gain * jnp.repeat(jnp.exp(draws), shape[position] // shards_of).reshape((-1,) + (1,) * (len(shape) - 1 - position))
    return gain


def normal_values(stream_key, dims, deviation, bound, cuts=(), held_as=jnp.bfloat16):
    values = deviation * jax.random.normal(stream_key, dims, jnp.float32)
    if cuts:
        values = values * level_of(stream_key, dims, cuts, -0.22, 0.18)
    return jnp.clip(values, -bound, bound).astype(held_as)


def setup_inputs(seed: int = 0) -> dict:
    arg_keys = jax.random.split(jax.random.key(seed), 6)
    qkv = normal_values(arg_keys[0], (STREAMS, 3, C, LENGTH), 1.0, 6.0, ((0, 4), (3, 8)))
    taps = normal_values(arg_keys[1], (3, 3, C), 0.7, 3.5, ((2, 8),), jnp.float32)
    rate_table = draw_rate_table(jax.random.fold_in(arg_keys[5], 71), 0)
    residue_table = draw_residue_table(jax.random.fold_in(arg_keys[5], 71), 0)
    bias = jnp.clip(jax.random.uniform(arg_keys[4], (C,), jnp.float32, -0.5, 0.5) * level_of(arg_keys[4], (C,), ((0, 8),), -0.4, 0.0), -0.5, 0.5)
    return {"qkv": qkv, "taps": taps, "rate_table": rate_table, "residue_table": residue_table, "bias": bias}


def reference(qkv, taps, rate_table, residue_table, bias):
    hi = lax.Precision.HIGHEST
    x = qkv.astype(jnp.float32)
    zero = jnp.zeros(x.shape[:-1] + (1,), jnp.float32)
    one_back = jnp.concatenate([zero, x[..., :-1]], axis=-1)
    two_back = jnp.concatenate([zero, zero, x[..., :-2]], axis=-1)
    filtered = taps[0][None, :, :, None] * x + taps[1][None, :, :, None] * one_back + taps[2][None, :, :, None] * two_back
    gated = (filtered[:, 1] * filtered[:, 2]).astype(jnp.bfloat16)
    coef = residue_table * jnp.sqrt(2.0 * rate_table / ORDER)
    streams, chans, length = gated.shape
    group = min(64, chans)
    count = chans // group
    gated_f = gated.astype(jnp.float32)
    zb = gated_f.reshape(streams, count, group, length).transpose(1, 0, 2, 3)
    rb = rate_table.reshape(ORDER, count, group).transpose(1, 0, 2)
    cb = coef.reshape(ORDER, count, group).transpose(1, 0, 2)
    lag = jnp.arange(length).astype(jnp.float32)

    def one_group(items):
        zg, rg, cg = items
        kernel = jnp.einsum('nc,nct->ct', cg, jnp.exp(-rg[:, :, None] * lag), precision=hi)
        size = 2 * length
        spec = jnp.fft.rfft(zg, size, axis=-1) * jnp.fft.rfft(kernel, size, axis=-1)[None]
        return jnp.fft.irfft(spec, size, axis=-1)[..., :length]
    conv = lax.map(one_group, (zb, rb, cb))
    conv = conv.transpose(1, 0, 2, 3).reshape(streams, chans, length)
    long = (conv + bias[None, :, None] * gated_f).astype(jnp.bfloat16)
    return (filtered[:, 0] * long.astype(jnp.float32)).astype(jnp.bfloat16)
```

```python
import functools
import jax
import jax.numpy as jnp
from jax import lax
from jax.experimental import pallas as pl
from jax.experimental.pallas import tpu as pltpu
from jax.sharding import PartitionSpec as P

ORDER = 16
LANES = 128
SUB = 8
GROUP = LANES * SUB


def identity(size):
    rows = lax.broadcasted_iota(jnp.int32, (size, size), 0)
    columns = lax.broadcasted_iota(jnp.int32, (size, size), 1)
    return (rows == columns).astype(jnp.bfloat16)


def flipped(eye, block):
    return lax.dot_general(
        eye, block, (((1,), (1,)), ((), ())), preferred_element_type=jnp.float32
    )


def to_tokens(eye, source, target, blocks, group, tokens):
    for sub in range(SUB):
        block = group * SUB + sub
        tile = source[pl.ds(pl.multiple_of(block * LANES, LANES), LANES), :]
        target[pl.ds(2 * blocks + block, tokens, stride=blocks), :] = flipped(eye, tile)


def rows_at(ref, token, blocks, group):
    return ref[pl.ds(pl.multiple_of(token * blocks + group * SUB, SUB), SUB), :]


def rounded(value):
    return value.astype(jnp.bfloat16).astype(jnp.float32)


def tree_sum(terms):
    terms = list(terms)
    while len(terms) > 1:
        terms = [a + b for a, b in zip(terms[::2], terms[1::2])]
    return terms[0]


def local_kernel(blocks, tokens, kv, halo, taps, bias, decay, coef, y_ref, s_ref, k_s, v_s):
    eye = identity(tokens)
    k_s[0 : 2 * blocks, :] = halo[1]
    v_s[0 : 2 * blocks, :] = halo[2]

    def one_group(group, _):
        to_tokens(eye, kv.at[1], k_s, blocks, group, tokens)
        to_tokens(eye, kv.at[2], v_s, blocks, group, tokens)
        own = pl.ds(pl.multiple_of(group * SUB, SUB), SUB)
        tap = [[taps[i, w, own, :] for i in range(3)] for w in (1, 2)]
        direct = bias[own, :]
        dec = [decay[n, own, :] for n in range(ORDER)]
        coe = [coef[n, own, :] for n in range(ORDER)]

        def step(t, carry):
            k2, k1, v2, v1, states = carry
            k0 = rows_at(k_s, t + 2, blocks, group)
            v0 = rows_at(v_s, t + 2, blocks, group)
            fk = tap[0][0] * k0 + tap[0][1] * k1 + tap[0][2] * k2
            fv = tap[1][0] * v0 + tap[1][1] * v1 + tap[1][2] * v2
            u = rounded(fk * fv)
            states = tuple(d * s + u for d, s in zip(dec, states))
            y = tree_sum(c * s for c, s in zip(coe, states)) + direct * u
            y_ref[pl.ds(pl.multiple_of(t * blocks + group * SUB, SUB), SUB), :] = y
            return (k1, k0, v1, v0, states)

        zero = jnp.zeros((SUB, LANES), jnp.float32)
        start = (
            rows_at(k_s, 0, blocks, group),
            rows_at(k_s, 1, blocks, group),
            rows_at(v_s, 0, blocks, group),
            rows_at(v_s, 1, blocks, group),
            (zero,) * ORDER,
        )
        states = lax.fori_loop(0, tokens, step, start, unroll=4)[4]
        for n in range(ORDER):
            s_ref[n, own, :] = states[n]
        return 0

    lax.fori_loop(0, blocks // SUB, one_group, 0)


def final_kernel(blocks, tokens, qkv, halo, taps, decay, coef, carry, y_ref, out, q_s):
    eye = identity(tokens)
    q_s[0 : 2 * blocks, :] = halo[0]

    def one_group(group, _):
        to_tokens(eye, qkv.at[0], q_s, blocks, group, tokens)
        own = pl.ds(pl.multiple_of(group * SUB, SUB), SUB)
        tap = [taps[i, 0, own, :] for i in range(3)]
        dec = [decay[n, own, :] for n in range(ORDER)]
        first = tuple(coef[n, own, :] * carry[n, own, :] for n in range(ORDER))

        def step(t, state):
            q2, q1, parts = state
            q0 = rows_at(q_s, t + 2, blocks, group)
            parts = tuple(d * z for d, z in zip(dec, parts))
            long = rounded(rows_at(y_ref, t, blocks, group) + tree_sum(parts))
            fq = tap[0] * q0 + tap[1] * q1 + tap[2] * q2
            q_s[pl.ds(pl.multiple_of(t * blocks + group * SUB, SUB), SUB), :] = fq * long
            return (q1, q0, parts)

        lax.fori_loop(
            0,
            tokens,
            step,
            (rows_at(q_s, 0, blocks, group), rows_at(q_s, 1, blocks, group), first),
            unroll=4,
        )
        for sub in range(SUB):
            block = group * SUB + sub
            tile = q_s[pl.ds(block, tokens, stride=blocks), :].astype(jnp.bfloat16)
            out[pl.ds(pl.multiple_of(block * LANES, LANES), LANES), :] = flipped(eye, tile).astype(
                jnp.bfloat16
            )
        return 0

    lax.fori_loop(0, blocks // SUB, one_group, 0)


def gathered(taps, rate_table, residue_table, bias, dp, ctx):
    modes, width = rate_table.shape
    rows = -(-10 // dp)
    extra = jnp.concatenate(
        [taps.reshape(9, width), bias[None], jnp.zeros((rows * dp - 10, width), jnp.float32)]
    )
    own = lax.dynamic_slice_in_dim(extra, lax.axis_index("dp") * rows, rows, 0)
    packed = jnp.concatenate([rate_table, residue_table, own])
    whole = lax.all_gather(packed, ("dp", "ctx"), axis=0)
    height = 2 * modes + rows
    whole = whole.reshape(dp, ctx, height, width).transpose(0, 2, 1, 3)
    whole = whole.reshape(dp, height, ctx * width // LANES, LANES)
    blocks = whole.shape[2]
    rate = whole[:, :modes].reshape(dp * modes, blocks, LANES)
    residue = whole[:, modes : 2 * modes].reshape(dp * modes, blocks, LANES)
    rest = whole[:, 2 * modes :].reshape(dp * rows, blocks, LANES)
    return rate, residue, rest[:9].reshape(3, 3, blocks, LANES), rest[9]


def per_device(dp, ctx, qkv, taps, rate_table, residue_table, bias):
    _, _, chans, tokens = qkv.shape
    blocks = chans // LANES
    own = qkv[0]
    halo = jnp.transpose(own[:, :, tokens - 2 :], (0, 2, 1)).reshape(3, 2 * blocks, LANES)
    halo = lax.ppermute(halo, "ctx", [(i, i + 1) for i in range(ctx - 1)]).astype(jnp.float32)
    rate, residue, taps, bias = gathered(taps, rate_table, residue_table, bias, dp, ctx)
    coef = residue * jnp.sqrt(2.0 * rate / ORDER)
    decay = jnp.exp(-rate)
    vmem = pl.BlockSpec(memory_space=pltpu.VMEM)
    params = pltpu.CompilerParams(vmem_limit_bytes=40 * 1024 * 1024)
    wide = (tokens + 2) * blocks
    y, last = pl.pallas_call(
        functools.partial(local_kernel, blocks, tokens),
        out_shape=(
            jax.ShapeDtypeStruct((tokens * blocks, LANES), jnp.float32),
            jax.ShapeDtypeStruct((ORDER, blocks, LANES), jnp.float32),
        ),
        in_specs=[vmem] * 6,
        out_specs=(vmem, vmem),
        scratch_shapes=[pltpu.VMEM((wide, LANES), jnp.float32)] * 2,
        compiler_params=params,
    )(own, halo, taps, bias, decay, coef)

    block_decay = jnp.exp(-rate * tokens)
    carry = jnp.zeros_like(last)
    reach = 1
    while reach < ctx:
        window = last + block_decay * carry if reach > 1 else last
        moved = lax.ppermute(window, "ctx", [(i, i + reach) for i in range(ctx - reach)])
        carry = carry + jnp.exp(-rate * (tokens * (reach - 1.0))) * moved
        reach *= 2

    out = pl.pallas_call(
        functools.partial(final_kernel, blocks, tokens),
        out_shape=jax.ShapeDtypeStruct((chans, tokens), jnp.bfloat16),
        in_specs=[vmem] * 7,
        out_specs=vmem,
        scratch_shapes=[pltpu.VMEM((wide, LANES), jnp.float32)],
        compiler_params=params,
    )(own, halo, taps, decay, coef, carry, y)
    return out[None]


def solution(mesh):
    in_specs = (
        P("dp", None, None, "ctx"),
        P(None, None, "ctx"),
        P("dp", "ctx"),
        P("dp", "ctx"),
        P("ctx"),
    )
    return jax.shard_map(
        functools.partial(per_device, mesh.shape["dp"], mesh.shape["ctx"]),
        mesh=mesh,
        in_specs=in_specs,
        out_specs=P("dp", None, "ctx"),
        check_vma=False,
    )
```

```python
import functools
import jax
import jax.numpy as jnp
from jax import lax
from jax.experimental import pallas as pl
from jax.experimental.pallas import tpu as pltpu
from jax.sharding import PartitionSpec as P

ORDER = 16
LANES = 128
SUB = 8
GROUP = LANES * SUB


def identity(size):
    rows = lax.broadcasted_iota(jnp.int32, (size, size), 0)
    columns = lax.broadcasted_iota(jnp.int32, (size, size), 1)
    return (rows == columns).astype(jnp.bfloat16)


def flipped(eye, block):
    return lax.dot_general(
        eye, block, (((1,), (1,)), ((), ())), preferred_element_type=jnp.float32
    )


def to_tokens(eye, source, target, blocks, group, tokens):
    for sub in range(SUB):
        block = group * SUB + sub
        tile = source[pl.ds(pl.multiple_of(block * LANES, LANES), LANES), :]
        target[pl.ds(2 * blocks + block, tokens, stride=blocks), :] = flipped(eye, tile)


def rows_at(ref, token, blocks, group):
    return ref[pl.ds(pl.multiple_of(token * blocks + group * SUB, SUB), SUB), :]


def rounded(value):
    return value.astype(jnp.bfloat16).astype(jnp.float32)


def tree_sum(terms):
    terms = list(terms)
    while len(terms) > 1:
        terms = [a + b for a, b in zip(terms[::2], terms[1::2])]
    return terms[0]


MESH = pl.DeviceIdType.MESH


def mixer_kernel(dp, ctx, blocks, tokens, inside, rows, *refs):
    qkv, given, out = refs[:3]
    q_s, k_s, v_s, y_s, held, table, last, window, came, carry = refs[3:13]
    par_send, par_recv, dp_send, dp_recv, halo_send, halo_recv, step_send, step_recv = refs[13:]
    me = lax.axis_index("ctx")
    own_dp = lax.axis_index("dp")
    groups = blocks // SUB
    reaches = [1 << s for s in range((ctx - 1).bit_length())]
    modes = ORDER // dp
    height = 2 * modes + rows
    across = lax.rem(own_dp + dp // 2, dp)
    beside = own_dp + 1 - 2 * lax.rem(own_dp, 2)

    barrier = pltpu.get_barrier_semaphore()

    def greet(k, _):
        pl.semaphore_signal(
            barrier, inc=1, device_id={"ctx": lax.rem(me + k, ctx)}, device_id_type=MESH
        )
        return 0

    lax.fori_loop(1, ctx, greet, 0)
    greeted = ctx - 1
    if inside:
        for other in (across, beside):
            pl.semaphore_signal(barrier, inc=1, device_id={"dp": other}, device_id_type=MESH)
        greeted += 2
    pl.semaphore_wait(barrier, greeted)

    def remote(source, target, send, recv, where):
        return pltpu.make_async_remote_copy(
            src_ref=source,
            dst_ref=target,
            send_sem=send,
            recv_sem=recv,
            device_id=where,
            device_id_type=MESH,
        )

    def share(k):
        to = {"ctx": lax.rem(me + k, ctx)}
        return remote(given, held.at[own_dp, me], par_send.at[k], par_recv.at[k], to)

    def start_share(k, _):
        share(k).start()
        return 0

    def wait_share(k, _):
        share(k).wait()
        return 0

    if inside:
        lax.fori_loop(1, ctx, start_share, 0)
        held[own_dp, me] = given[...]

    eye = identity(tokens)

    def turn(group, _):
        to_tokens(eye, qkv.at[0], q_s, blocks, group, tokens)
        to_tokens(eye, qkv.at[1], k_s, blocks, group, tokens)
        to_tokens(eye, qkv.at[2], v_s, blocks, group, tokens)
        return 0

    lax.fori_loop(0, groups, turn, 0)

    streams = (q_s, k_s, v_s)
    ends = [
        remote(
            ref.at[pl.ds(tokens * blocks, 2 * blocks), :],
            ref.at[pl.ds(0, 2 * blocks), :],
            halo_send.at[w],
            halo_recv.at[w],
            {"ctx": lax.rem(me + 1, ctx)},
        )
        for w, ref in enumerate(streams)
    ]

    @pl.when(me + 1 < ctx)
    def _():
        for copy in ends:
            copy.start()

    @pl.when(me == 0)
    def _():
        for ref in streams:
            ref[0 : 2 * blocks, :] = jnp.zeros((2 * blocks, LANES), jnp.float32)

    for s, reach in enumerate(reaches):

        @pl.when(me < reach)
        def _(s=s):
            came[s] = jnp.zeros_like(came[s])

    if inside:
        lax.fori_loop(1, ctx, wait_share, 0)
        part = held.at[own_dp]
        far = remote(part, part, dp_send.at[0], dp_recv.at[0], {"dp": across})
        near = remote(part, part, dp_send.at[1], dp_recv.at[1], {"dp": beside})
        far.start()
        near.start()
        far.wait()
        other = held.at[across]
        last_part = remote(other, other, dp_send.at[2], dp_recv.at[2], {"dp": beside})
        last_part.start()
        near.wait()
        last_part.wait()
        each = blocks // ctx

        def place(d, _):
            for c in range(ctx):
                for h in range(height):
                    table[d * height + h, each * c : each * (c + 1), :] = held[
                        d, c, each * h : each * (h + 1), :
                    ]
            return 0

        lax.fori_loop(0, dp, place, 0)
        source = table
    else:
        source = given

    @pl.when(me > 0)
    def _():
        for copy in ends:
            copy.wait_recv()

    def owned(group):
        return pl.ds(group * SUB, SUB)

    def rate_of(n, group):
        return source[(n // modes) * height + n % modes, owned(group), :]

    def coef_of(n, group):
        residue = source[(n // modes) * height + modes + n % modes, owned(group), :]
        return residue * jnp.sqrt(2.0 * rate_of(n, group) / ORDER)

    def extra(e, group):
        return source[(e // rows) * height + 2 * modes + e % rows, owned(group), :]

    def step_copy(s, group):
        ref = last.at[group] if s == 0 else window.at[s - 1, group]
        return remote(
            ref,
            came.at[s, group],
            step_send.at[s, group],
            step_recv.at[s, group],
            {"ctx": lax.rem(me + reaches[s], ctx)},
        )

    def send(s, group):
        @pl.when(me + reaches[s] < ctx)
        def _():
            step_copy(s, group).start()

    def scan(group):
        tap = [[extra(3 * i + w, group) for i in range(3)] for w in (1, 2)]
        direct = extra(9, group)
        dec = [jnp.exp(-rate_of(n, group)) for n in range(ORDER)]
        coe = [coef_of(n, group) for n in range(ORDER)]

        def step(t, state):
            k2, k1, v2, v1, states = state
            k0 = rows_at(k_s, t + 2, blocks, group)
            v0 = rows_at(v_s, t + 2, blocks, group)
            fk = tap[0][0] * k0 + tap[0][1] * k1 + tap[0][2] * k2
            fv = tap[1][0] * v0 + tap[1][1] * v1 + tap[1][2] * v2
            u = rounded(fk * fv)
            states = tuple(d * s + u for d, s in zip(dec, states))
            y = tree_sum(c * s for c, s in zip(coe, states)) + direct * u
            y_s[pl.ds(pl.multiple_of(t * blocks + group * SUB, SUB), SUB), :] = y
            return (k1, k0, v1, v0, states)

        zero = jnp.zeros((SUB, LANES), jnp.float32)
        start = (
            rows_at(k_s, 0, blocks, group),
            rows_at(k_s, 1, blocks, group),
            rows_at(v_s, 0, blocks, group),
            rows_at(v_s, 1, blocks, group),
            (zero,) * ORDER,
        )
        states = lax.fori_loop(0, tokens, step, start, unroll=4)[4]
        for n in range(ORDER):
            last[group, n] = states[n]
        send(0, group)

    def combine(s, group):
        @pl.when(me >= reaches[s])
        def _():
            step_copy(s, group).wait_recv()

        for n in range(ORDER):
            rate = rate_of(n, group)
            total = came[s, group, n]
            if s > 0:
                past = jnp.exp(-rate * (tokens * (reaches[s] - 1.0)))
                total = carry[group, n] + past * total
            carry[group, n] = total
            if s + 1 < len(reaches):
                window[s, group, n] = last[group, n] + jnp.exp(-rate * tokens) * total
        if s + 1 < len(reaches):
            send(s + 1, group)

    def finish(group):
        tap = [extra(3 * i, group) for i in range(3)]
        dec = [jnp.exp(-rate_of(n, group)) for n in range(ORDER)]
        first = tuple(coef_of(n, group) * carry[group, n] for n in range(ORDER))

        def step(t, state):
            q2, q1, parts = state
            q0 = rows_at(q_s, t + 2, blocks, group)
            parts = tuple(d * z for d, z in zip(dec, parts))
            long = rounded(rows_at(y_s, t, blocks, group) + tree_sum(parts))
            fq = tap[0] * q0 + tap[1] * q1 + tap[2] * q2
            y_s[pl.ds(pl.multiple_of(t * blocks + group * SUB, SUB), SUB), :] = fq * long
            return (q1, q0, parts)

        start = (rows_at(q_s, 0, blocks, group), rows_at(q_s, 1, blocks, group), first)
        lax.fori_loop(0, tokens, step, start, unroll=4)
        for sub in range(SUB):
            block = group * SUB + sub
            tile = y_s[pl.ds(block, tokens, stride=blocks), :].astype(jnp.bfloat16)
            out[block * LANES : (block + 1) * LANES, :] = flipped(eye, tile).astype(jnp.bfloat16)

    for group in range(groups):
        scan(group)
        if group > 0:
            combine(0, group - 1)
    combine(0, groups - 1)
    for s in range(1, len(reaches) - 1):
        for group in range(groups):
            combine(s, group)
    for group in range(groups):
        if len(reaches) > 1:
            combine(len(reaches) - 1, group)
        finish(group)

    @pl.when(me + 1 < ctx)
    def _():
        for copy in ends:
            copy.wait_send()

    for s, reach in enumerate(reaches):

        @pl.when(me + reach < ctx)
        def _(s=s):
            for group in range(groups):
                step_copy(s, group).wait_send()


def local_pack(taps, rate_table, residue_table, bias, dp):
    width = bias.shape[0]
    rows = -(-10 // dp)
    extra = jnp.concatenate(
        [taps.reshape(9, width), bias[None], jnp.zeros((rows * dp - 10, width), jnp.float32)]
    )
    own = lax.dynamic_slice_in_dim(extra, lax.axis_index("dp") * rows, rows, 0)
    return jnp.concatenate([rate_table, residue_table, own])


def gathered(packed, dp, ctx):
    height, width = packed.shape
    whole = lax.all_gather(packed, ("dp", "ctx"), axis=0)
    whole = whole.reshape(dp, ctx, height, width).transpose(0, 2, 1, 3)
    return whole.reshape(dp * height, ctx * width // LANES, LANES)


def per_device(dp, ctx, qkv, taps, rate_table, residue_table, bias):
    _, _, chans, tokens = qkv.shape
    blocks = chans // LANES
    modes, width = rate_table.shape
    rows = -(-10 // dp)
    height = 2 * modes + rows
    inside = dp == 4 and width % LANES == 0
    packed = local_pack(taps, rate_table, residue_table, bias, dp)
    if inside:
        given = packed.reshape(height * width // LANES, LANES)
    else:
        given = gathered(packed, dp, ctx)
    groups = blocks // SUB
    steps = (ctx - 1).bit_length()
    wide = (tokens + 2) * blocks
    each = height * max(width // LANES, 1) if inside else 8
    vmem = pl.BlockSpec(memory_space=pltpu.VMEM)
    slab = (groups, ORDER, SUB, LANES)
    f32 = jnp.float32
    out = pl.pallas_call(
        functools.partial(mixer_kernel, dp, ctx, blocks, tokens, inside, rows),
        out_shape=jax.ShapeDtypeStruct((chans, tokens), jnp.bfloat16),
        in_specs=[vmem] * 2,
        out_specs=vmem,
        scratch_shapes=[
            pltpu.VMEM((wide, LANES), f32),
            pltpu.VMEM((wide, LANES), f32),
            pltpu.VMEM((wide, LANES), f32),
            pltpu.VMEM((tokens * blocks, LANES), f32),
            pltpu.VMEM((dp, ctx, each, LANES) if inside else (1, 1, each, LANES), f32),
            pltpu.VMEM((dp * height, blocks, LANES) if inside else (1, SUB, LANES), f32),
            pltpu.VMEM(slab, f32),
            pltpu.VMEM((max(steps - 1, 1),) + slab, f32),
            pltpu.VMEM((steps,) + slab, f32),
            pltpu.VMEM(slab, f32),
            pltpu.SemaphoreType.DMA((ctx,)),
            pltpu.SemaphoreType.DMA((ctx,)),
            pltpu.SemaphoreType.DMA((3,)),
            pltpu.SemaphoreType.DMA((3,)),
            pltpu.SemaphoreType.DMA((3,)),
            pltpu.SemaphoreType.DMA((3,)),
            pltpu.SemaphoreType.DMA((steps, groups)),
            pltpu.SemaphoreType.DMA((steps, groups)),
        ],
        compiler_params=pltpu.CompilerParams(
            collective_id=0, has_side_effects=True, vmem_limit_bytes=48 * 1024 * 1024
        ),
    )(qkv[0], given)
    return out[None]


def solution(mesh):
    in_specs = (
        P("dp", None, None, "ctx"),
        P(None, None, "ctx"),
        P("dp", "ctx"),
        P("dp", "ctx"),
        P("ctx"),
    )
    return jax.shard_map(
        functools.partial(per_device, mesh.shape["dp"], mesh.shape["ctx"]),
        mesh=mesh,
        in_specs=in_specs,
        out_specs=P("dp", None, "ctx"),
        check_vma=False,
    )
```

```python
import functools
import jax
import jax.numpy as jnp
from jax import lax
from jax.experimental import pallas as pl
from jax.experimental.pallas import tpu as pltpu
from jax.sharding import PartitionSpec as P

ORDER = 16
LANES = 128
SUB = 8
GROUP = LANES * SUB


def identity(size):
    rows = lax.broadcasted_iota(jnp.int32, (size, size), 0)
    columns = lax.broadcasted_iota(jnp.int32, (size, size), 1)
    return (rows == columns).astype(jnp.bfloat16)


def flipped(eye, block):
    return lax.dot_general(
        eye, block, (((1,), (1,)), ((), ())), preferred_element_type=jnp.float32
    )


def to_tokens(eye, source, target, blocks, group, tokens):
    for sub in range(SUB):
        block = group * SUB + sub
        tile = source[pl.ds(block * LANES, LANES), :]
        target[pl.ds(2 * blocks + block, tokens, stride=blocks), :] = flipped(eye, tile)


def rows_at(ref, token, blocks, group):
    return ref[pl.ds(pl.multiple_of(token * blocks + group * SUB, SUB), SUB), :]


def rounded(value):
    return value.astype(jnp.bfloat16).astype(jnp.float32)


def tree_sum(terms):
    terms = list(terms)
    while len(terms) > 1:
        terms = [a + b for a, b in zip(terms[::2], terms[1::2])]
    return terms[0]


MESH = pl.DeviceIdType.MESH


def mixer_kernel(dp, ctx, blocks, tokens, inside, rows, *refs):
    qkv, given, out = refs[:3]
    raw, q_s, k_s, v_s, y_s, held, table, last, window, came, carry, load = refs[3:15]
    par_send, par_recv, dp_send, dp_recv, halo_send, halo_recv, step_send, step_recv = refs[15:]
    me = lax.axis_index("ctx")
    own_dp = lax.axis_index("dp")
    groups = blocks // SUB
    steps = (ctx - 1).bit_length()
    pair = lax.div(me, 2)
    second = lax.rem(me, 2)
    modes = ORDER // dp
    height = 2 * modes + rows
    across = lax.rem(own_dp + dp // 2, dp)
    beside = own_dp + 1 - 2 * lax.rem(own_dp, 2)

    def fetch(group):
        own = pl.ds(group * GROUP, GROUP)
        return pltpu.make_async_copy(qkv.at[:, own, :], raw.at[:, own, :], load.at[group])

    for group in range(groups):
        fetch(group).start()

    barrier = pltpu.get_barrier_semaphore()

    def greet(k, _):
        pl.semaphore_signal(
            barrier, inc=1, device_id={"ctx": lax.rem(me + k, ctx)}, device_id_type=MESH
        )
        return 0

    lax.fori_loop(1, ctx, greet, 0)
    greeted = ctx - 1
    if inside:
        for other in (across, beside):
            pl.semaphore_signal(barrier, inc=1, device_id={"dp": other}, device_id_type=MESH)
        greeted += 2
    pl.semaphore_wait(barrier, greeted)

    def remote(source, target, send, recv, where):
        return pltpu.make_async_remote_copy(
            src_ref=source,
            dst_ref=target,
            send_sem=send,
            recv_sem=recv,
            device_id=where,
            device_id_type=MESH,
        )

    def share(k):
        to = {"ctx": lax.rem(me + k, ctx)}
        return remote(given, held.at[own_dp, me], par_send.at[k], par_recv.at[k], to)

    def start_share(k, _):
        share(k).start()
        return 0

    def relay(hop, k):
        from_dp = across if hop == 2 else own_dp
        block = held.at[from_dp, lax.rem(me + ctx - k, ctx)]
        to = across if hop == 0 else beside
        return remote(block, block, dp_send.at[hop, k], dp_recv.at[hop, k], {"dp": to})

    def pass_on(k, _):
        if not isinstance(k, int):
            share(k).wait_recv()
        relay(0, k).start()
        relay(1, k).start()
        return 0

    def pass_far(k, _):
        relay(0, k).wait_recv()
        relay(2, k).start()
        return 0

    def arrive(k, _):
        relay(1, k).wait_recv()
        relay(2, k).wait_recv()
        return 0

    def all_sent(k, _):
        for hop in range(3):
            relay(hop, k).wait_send()
        return 0

    def share_sent(k, _):
        share(k).wait_send()
        return 0

    if inside:
        lax.fori_loop(1, ctx, start_share, 0)
        held[own_dp, me] = given[...]
        pass_on(0, 0)

    eye = identity(tokens)

    for group in range(groups):
        fetch(group).wait()
        to_tokens(eye, raw.at[1], k_s, blocks, group, tokens)
        to_tokens(eye, raw.at[2], v_s, blocks, group, tokens)
        to_tokens(eye, raw.at[0], q_s, blocks, group, tokens)
        if inside and group == groups // 2 - 1:
            lax.fori_loop(1, ctx, pass_on, 0)

    streams = (q_s, k_s, v_s)
    ends = [
        remote(
            ref.at[pl.ds(tokens * blocks, 2 * blocks), :],
            ref.at[pl.ds(0, 2 * blocks), :],
            halo_send.at[w],
            halo_recv.at[w],
            {"ctx": lax.rem(me + 1, ctx)},
        )
        for w, ref in enumerate(streams)
    ]

    @pl.when(me + 1 < ctx)
    def _():
        for copy in ends:
            copy.start()

    @pl.when(me == 0)
    def _():
        for ref in streams:
            ref[0 : 2 * blocks, :] = jnp.zeros((2 * blocks, LANES), jnp.float32)

    def sends(s):
        return lax.rem(pair, 1 << s) == (1 << (s - 1)) - 1

    def takes(s):
        return lax.rem(pair, 1 << s) >= 1 << (s - 1)

    for s in range(1, steps):

        @pl.when(jnp.logical_not(takes(s)))
        def _(s=s):
            came[s] = jnp.zeros_like(came[s])

    if inside:
        lax.fori_loop(0, ctx, pass_far, 0)
        lax.fori_loop(0, ctx, arrive, 0)
        each = blocks // ctx

        def place(d, _):
            for c in range(ctx):
                for h in range(height):
                    table[d * height + h, each * c : each * (c + 1), :] = held[
                        d, c, each * h : each * (h + 1), :
                    ]
            return 0

        lax.fori_loop(0, dp, place, 0)
        source = table
    else:
        source = given

    @pl.when(me > 0)
    def _():
        for copy in ends:
            copy.wait_recv()

    def owned(group):
        return pl.ds(group * SUB, SUB)

    def rate_of(n, group):
        return source[(n // modes) * height + n % modes, owned(group), :]

    def coef_of(n, group):
        residue = source[(n // modes) * height + modes + n % modes, owned(group), :]
        return residue * jnp.sqrt(2.0 * rate_of(n, group) / ORDER)

    def extra(e, group):
        return source[(e // rows) * height + 2 * modes + e % rows, owned(group), :]

    def swap(group):
        return remote(
            last.at[group],
            came.at[0, group],
            step_send.at[0, group],
            step_recv.at[0, group],
            {"ctx": me + 1 - 2 * second},
        )

    def spread(s, j, group):
        return remote(
            window.at[s - 1, group],
            came.at[s, group],
            step_send.at[(1 << (s - 1)) + j, group],
            step_recv.at[s, group],
            {"ctx": lax.rem(me + 2 * (j + 1), ctx)},
        )

    def scan(group):
        tap = [[extra(3 * i + w, group) for i in range(3)] for w in (1, 2)]
        direct = extra(9, group)
        dec = [jnp.exp(-rate_of(n, group)) for n in range(ORDER)]
        coe = [coef_of(n, group) for n in range(ORDER)]

        def step(t, state):
            k2, k1, v2, v1, states = state
            k0 = rows_at(k_s, t + 2, blocks, group)
            v0 = rows_at(v_s, t + 2, blocks, group)
            fk = tap[0][0] * k0 + tap[0][1] * k1 + tap[0][2] * k2
            fv = tap[1][0] * v0 + tap[1][1] * v1 + tap[1][2] * v2
            u = rounded(fk * fv)
            states = tuple(d * s + u for d, s in zip(dec, states))
            y = tree_sum(c * s for c, s in zip(coe, states)) + direct * u
            y_s[pl.ds(pl.multiple_of(t * blocks + group * SUB, SUB), SUB), :] = y
            return (k1, k0, v1, v0, states)

        zero = jnp.zeros((SUB, LANES), jnp.float32)
        start = (
            rows_at(k_s, 0, blocks, group),
            rows_at(k_s, 1, blocks, group),
            rows_at(v_s, 0, blocks, group),
            rows_at(v_s, 1, blocks, group),
            (zero,) * ORDER,
        )
        states = lax.fori_loop(0, tokens, step, start, unroll=4)[4]
        for n in range(ORDER):
            last[group, n] = states[n]
        swap(group).start()

    def combine(s, group):
        if s == 0:
            swap(group).wait_recv()
        else:

            @pl.when(takes(s))
            def _():
                spread(s, 0, group).wait_recv()

            ahead = jnp.maximum(lax.rem(pair, 1 << s) - (1 << (s - 1)), 0)
            ahead = ahead.astype(jnp.float32) * (2.0 * tokens)
        for n in range(ORDER):
            rate = rate_of(n, group)
            if s == 0:
                mine, other = last[group, n], came[0, group, n]
                first = jnp.where(second == 0, mine, other)
                later = jnp.where(second == 0, other, mine)
                window[0, group, n] = later + jnp.exp(-rate * tokens) * first
            else:
                total = jnp.exp(-rate * ahead) * came[s, group, n]
                if s > 1:
                    total = total + carry[group, n]
                if s + 1 < steps:
                    within = jnp.exp(-rate * (2.0 * tokens)) * total
                    window[s, group, n] = window[0, group, n] + within
                    carry[group, n] = total
                else:
                    behind = came[0, group, n] + jnp.exp(-rate * tokens) * total
                    carry[group, n] = jnp.where(second == 0, total, behind)
        if s + 1 < steps:

            @pl.when(sends(s + 1))
            def _():
                for j in range(1 << s):
                    spread(s + 1, j, group).start()

    def finish(group):
        tap = [extra(3 * i, group) for i in range(3)]
        dec = [jnp.exp(-rate_of(n, group)) for n in range(ORDER)]
        first = tuple(coef_of(n, group) * carry[group, n] for n in range(ORDER))

        def step(t, state):
            q2, q1, parts = state
            q0 = rows_at(q_s, t + 2, blocks, group)
            parts = tuple(d * z for d, z in zip(dec, parts))
            long = rounded(rows_at(y_s, t, blocks, group) + tree_sum(parts))
            fq = tap[0] * q0 + tap[1] * q1 + tap[2] * q2
            y_s[pl.ds(pl.multiple_of(t * blocks + group * SUB, SUB), SUB), :] = fq * long
            return (q1, q0, parts)

        start = (rows_at(q_s, 0, blocks, group), rows_at(q_s, 1, blocks, group), first)
        lax.fori_loop(0, tokens, step, start, unroll=4)
        for sub in range(SUB):
            block = group * SUB + sub
            tile = y_s[pl.ds(block, tokens, stride=blocks), :].astype(jnp.bfloat16)
            out[block * LANES : (block + 1) * LANES, :] = flipped(eye, tile).astype(jnp.bfloat16)

    for group in range(groups):
        scan(group)
        for s in range(steps - 1):
            if group > s:
                combine(s, group - 1 - s)
    for late in range(groups, groups + steps - 1):
        for s in range(steps - 1):
            if 0 <= late - 1 - s < groups:
                combine(s, late - 1 - s)
    for group in range(groups):
        combine(steps - 1, group)
        finish(group)

    @pl.when(me + 1 < ctx)
    def _():
        for copy in ends:
            copy.wait_send()

    if inside:
        lax.fori_loop(1, ctx, share_sent, 0)
        lax.fori_loop(0, ctx, all_sent, 0)
    for group in range(groups):
        swap(group).wait_send()
    for s in range(1, steps):

        @pl.when(sends(s))
        def _(s=s):
            for j in range(1 << (s - 1)):
                for group in range(groups):
                    spread(s, j, group).wait_send()


def local_pack(taps, rate_table, residue_table, bias, dp):
    width = bias.shape[0]
    rows = -(-10 // dp)
    extra = jnp.concatenate(
        [taps.reshape(9, width), bias[None], jnp.zeros((rows * dp - 10, width), jnp.float32)]
    )
    own = lax.dynamic_slice_in_dim(extra, lax.axis_index("dp") * rows, rows, 0)
    return jnp.concatenate([rate_table, residue_table, own])


def gathered(packed, dp, ctx):
    height, width = packed.shape
    whole = lax.all_gather(packed, ("dp", "ctx"), axis=0)
    whole = whole.reshape(dp, ctx, height, width).transpose(0, 2, 1, 3)
    return whole.reshape(dp * height, ctx * width // LANES, LANES)


def per_device(dp, ctx, qkv, taps, rate_table, residue_table, bias):
    _, _, chans, tokens = qkv.shape
    blocks = chans // LANES
    modes, width = rate_table.shape
    rows = -(-10 // dp)
    height = 2 * modes + rows
    inside = dp == 4 and width % LANES == 0
    packed = local_pack(taps, rate_table, residue_table, bias, dp)
    if inside:
        given = packed.reshape(height * width // LANES, LANES)
    else:
        given = gathered(packed, dp, ctx)
    groups = blocks // SUB
    steps = (ctx - 1).bit_length()
    wide = (tokens + 2) * blocks
    each = height * max(width // LANES, 1) if inside else 8
    vmem = pl.BlockSpec(memory_space=pltpu.VMEM)
    slab = (groups, ORDER, SUB, LANES)
    f32 = jnp.float32
    out = pl.pallas_call(
        functools.partial(mixer_kernel, dp, ctx, blocks, tokens, inside, rows),
        out_shape=jax.ShapeDtypeStruct((chans, tokens), jnp.bfloat16),
        in_specs=[pl.BlockSpec(memory_space=pl.ANY), vmem],
        out_specs=vmem,
        scratch_shapes=[
            pltpu.VMEM((3, chans, tokens), jnp.bfloat16),
            pltpu.VMEM((wide, LANES), f32),
            pltpu.VMEM((wide, LANES), f32),
            pltpu.VMEM((wide, LANES), f32),
            pltpu.VMEM((tokens * blocks, LANES), f32),
            pltpu.VMEM((dp, ctx, each, LANES) if inside else (1, 1, each, LANES), f32),
            pltpu.VMEM((dp * height, blocks, LANES) if inside else (1, SUB, LANES), f32),
            pltpu.VMEM(slab, f32),
            pltpu.VMEM((max(steps - 1, 1),) + slab, f32),
            pltpu.VMEM((steps,) + slab, f32),
            pltpu.VMEM(slab, f32),
            pltpu.SemaphoreType.DMA((groups,)),
            pltpu.SemaphoreType.DMA((ctx,)),
            pltpu.SemaphoreType.DMA((ctx,)),
            pltpu.SemaphoreType.DMA((3, ctx if inside else 1)),
            pltpu.SemaphoreType.DMA((3, ctx if inside else 1)),
            pltpu.SemaphoreType.DMA((3,)),
            pltpu.SemaphoreType.DMA((3,)),
            pltpu.SemaphoreType.DMA((ctx // 2, groups)),
            pltpu.SemaphoreType.DMA((steps, groups)),
        ],
        compiler_params=pltpu.CompilerParams(
            collective_id=0, has_side_effects=True, vmem_limit_bytes=48 * 1024 * 1024
        ),
    )(qkv[0], given)
    return out[None]


def solution(mesh):
    in_specs = (
        P("dp", None, None, "ctx"),
        P(None, None, "ctx"),
        P("dp", "ctx"),
        P("dp", "ctx"),
        P("ctx"),
    )
    return jax.shard_map(
        functools.partial(per_device, mesh.shape["dp"], mesh.shape["ctx"]),
        mesh=mesh,
        in_specs=in_specs,
        out_specs=P("dp", None, "ctx"),
        check_vma=False,
    )
```

```python
import functools
import jax
import jax.numpy as jnp
from jax import lax
from jax.experimental import pallas as pl
from jax.experimental.pallas import tpu as pltpu
from jax.sharding import PartitionSpec as P

ORDER = 16
LANES = 128
SUB = 8
GROUP = LANES * SUB


def identity(size):
    rows = lax.broadcasted_iota(jnp.int32, (size, size), 0)
    columns = lax.broadcasted_iota(jnp.int32, (size, size), 1)
    return (rows == columns).astype(jnp.bfloat16)


def flipped(eye, block):
    return lax.dot_general(
        eye, block, (((1,), (1,)), ((), ())), preferred_element_type=jnp.float32
    )


def to_tokens(eye, source, target, blocks, group, tokens):
    for sub in range(SUB):
        block = group * SUB + sub
        tile = source[pl.ds(block * LANES, LANES), :]
        target[pl.ds(2 * blocks + block, tokens, stride=blocks), :] = flipped(eye, tile)


def rows_at(ref, token, blocks, group):
    return ref[pl.ds(pl.multiple_of(token * blocks + group * SUB, SUB), SUB), :]


def rounded(value):
    return value.astype(jnp.bfloat16).astype(jnp.float32)


def tree_sum(terms):
    terms = list(terms)
    while len(terms) > 1:
        terms = [a + b for a, b in zip(terms[::2], terms[1::2])]
    return terms[0]


MESH = pl.DeviceIdType.MESH


def mixer_kernel(dp, ctx, blocks, tokens, inside, rows, *refs):
    tables = 4 if inside else 1
    qkv, given = refs[0], refs[1 : 1 + tables]
    refs = refs[tables - 1 :]
    out = refs[2]
    raw, q_s, k_s, v_s, y_s, held, table, last, window, came, carry, load = refs[3:15]
    par_send, par_recv, dp_send, dp_recv, halo_send, halo_recv, step_send, step_recv = refs[15:]
    me = lax.axis_index("ctx")
    own_dp = lax.axis_index("dp")
    groups = blocks // SUB
    steps = (ctx - 1).bit_length()
    pair = lax.div(me, 2)
    second = lax.rem(me, 2)
    modes = ORDER // dp
    height = 2 * modes + rows
    across = lax.rem(own_dp + dp // 2, dp)
    beside = own_dp + 1 - 2 * lax.rem(own_dp, 2)

    def fetch(group):
        own = pl.ds(group * GROUP, GROUP)
        return pltpu.make_async_copy(qkv.at[:, own, :], raw.at[:, own, :], load.at[group])

    for group in range(groups):
        fetch(group).start()

    if inside:
        rate_in, residue_in, taps_in, bias_in = given
        each = blocks // ctx
        for b in range(each):
            lanes = slice(LANES * b, LANES * (b + 1))
            for h in range(modes):
                at = each * h + b
                held[own_dp, me, at : at + 1, :] = rate_in[h : h + 1, lanes]
                at += each * modes
                held[own_dp, me, at : at + 1, :] = residue_in[h : h + 1, lanes]
            for r in range(rows):
                line = bias_in[:, lanes]
                for d in range(dp):
                    e = d * rows + r
                    if e < 9:
                        tap = taps_in[e // 3, e % 3 : e % 3 + 1, lanes]
                        line = jnp.where(own_dp == d, tap, line)
                at = each * (2 * modes + r) + b
                held[own_dp, me, at : at + 1, :] = line

    barrier = pltpu.get_barrier_semaphore()

    def greet(k, _):
        pl.semaphore_signal(
            barrier, inc=1, device_id={"ctx": lax.rem(me + k, ctx)}, device_id_type=MESH
        )
        return 0

    lax.fori_loop(1, ctx, greet, 0)
    greeted = ctx - 1
    if inside:
        for other in (across, beside):
            pl.semaphore_signal(barrier, inc=1, device_id={"dp": other}, device_id_type=MESH)
        greeted += 2
    pl.semaphore_wait(barrier, greeted)

    def remote(source, target, send, recv, where):
        return pltpu.make_async_remote_copy(
            src_ref=source,
            dst_ref=target,
            send_sem=send,
            recv_sem=recv,
            device_id=where,
            device_id_type=MESH,
        )

    def share(k):
        to = {"ctx": lax.rem(me + k, ctx)}
        block = held.at[own_dp, me]
        return remote(block, block, par_send.at[k], par_recv.at[k], to)

    def start_share(k, _):
        share(k).start()
        return 0

    def relay(hop, k):
        from_dp = across if hop == 2 else own_dp
        block = held.at[from_dp, lax.rem(me + ctx - k, ctx)]
        to = across if hop == 0 else beside
        return remote(block, block, dp_send.at[hop, k], dp_recv.at[hop, k], {"dp": to})

    def pass_on(k, _):
        if not isinstance(k, int):
            share(k).wait_recv()
        relay(0, k).start()
        relay(1, k).start()
        return 0

    def pass_far(k, _):
        relay(0, k).wait_recv()
        relay(2, k).start()
        return 0

    def arrive(k, _):
        relay(1, k).wait_recv()
        relay(2, k).wait_recv()
        return 0

    def all_sent(k, _):
        for hop in range(3):
            relay(hop, k).wait_send()
        return 0

    def share_sent(k, _):
        share(k).wait_send()
        return 0

    if inside:
        lax.fori_loop(1, ctx, start_share, 0)
        pass_on(0, 0)

    eye = identity(tokens)

    for group in range(groups):
        fetch(group).wait()
        to_tokens(eye, raw.at[1], k_s, blocks, group, tokens)
        to_tokens(eye, raw.at[2], v_s, blocks, group, tokens)
        to_tokens(eye, raw.at[0], q_s, blocks, group, tokens)
        if inside and group == groups // 2 - 1:
            lax.fori_loop(1, ctx, pass_on, 0)

    streams = (q_s, k_s, v_s)
    ends = [
        remote(
            ref.at[pl.ds(tokens * blocks, 2 * blocks), :],
            ref.at[pl.ds(0, 2 * blocks), :],
            halo_send.at[w],
            halo_recv.at[w],
            {"ctx": lax.rem(me + 1, ctx)},
        )
        for w, ref in enumerate(streams)
    ]

    @pl.when(me + 1 < ctx)
    def _():
        for copy in ends:
            copy.start()

    @pl.when(me == 0)
    def _():
        for ref in streams:
            ref[0 : 2 * blocks, :] = jnp.zeros((2 * blocks, LANES), jnp.float32)

    def sends(s):
        return lax.rem(pair, 1 << s) == (1 << (s - 1)) - 1

    def takes(s):
        return lax.rem(pair, 1 << s) >= 1 << (s - 1)

    for s in range(1, steps):

        @pl.when(jnp.logical_not(takes(s)))
        def _(s=s):
            came[s] = jnp.zeros_like(came[s])

    if inside:
        lax.fori_loop(0, ctx, pass_far, 0)
        lax.fori_loop(0, ctx, arrive, 0)

        def place(d, _):
            for c in range(ctx):
                for h in range(height):
                    table[d * height + h, each * c : each * (c + 1), :] = held[
                        d, c, each * h : each * (h + 1), :
                    ]
            return 0

        lax.fori_loop(0, dp, place, 0)
        source = table
    else:
        source = given[0]

    @pl.when(me > 0)
    def _():
        for copy in ends:
            copy.wait_recv()

    def owned(group):
        return pl.ds(group * SUB, SUB)

    def rate_of(n, group):
        return source[(n // modes) * height + n % modes, owned(group), :]

    def coef_of(n, group):
        residue = source[(n // modes) * height + modes + n % modes, owned(group), :]
        return residue * jnp.sqrt(2.0 * rate_of(n, group) / ORDER)

    def extra(e, group):
        return source[(e // rows) * height + 2 * modes + e % rows, owned(group), :]

    def swap(group):
        return remote(
            last.at[group],
            came.at[0, group],
            step_send.at[0, group],
            step_recv.at[0, group],
            {"ctx": me + 1 - 2 * second},
        )

    def spread(s, j, group):
        return remote(
            window.at[s - 1, group],
            came.at[s, group],
            step_send.at[(1 << (s - 1)) + j, group],
            step_recv.at[s, group],
            {"ctx": lax.rem(me + 2 * (j + 1), ctx)},
        )

    def scan(group):
        tap = [[extra(3 * i + w, group) for i in range(3)] for w in (1, 2)]
        direct = extra(9, group)
        dec = [jnp.exp(-rate_of(n, group)) for n in range(ORDER)]
        coe = [coef_of(n, group) for n in range(ORDER)]

        def step(t, state):
            k2, k1, v2, v1, states = state
            k0 = rows_at(k_s, t + 2, blocks, group)
            v0 = rows_at(v_s, t + 2, blocks, group)
            fk = tap[0][0] * k0 + tap[0][1] * k1 + tap[0][2] * k2
            fv = tap[1][0] * v0 + tap[1][1] * v1 + tap[1][2] * v2
            u = rounded(fk * fv)
            states = tuple(d * s + u for d, s in zip(dec, states))
            y = tree_sum(c * s for c, s in zip(coe, states)) + direct * u
            y_s[pl.ds(pl.multiple_of(t * blocks + group * SUB, SUB), SUB), :] = y
            return (k1, k0, v1, v0, states)

        zero = jnp.zeros((SUB, LANES), jnp.float32)
        start = (
            rows_at(k_s, 0, blocks, group),
            rows_at(k_s, 1, blocks, group),
            rows_at(v_s, 0, blocks, group),
            rows_at(v_s, 1, blocks, group),
            (zero,) * ORDER,
        )
        states = lax.fori_loop(0, tokens, step, start, unroll=4)[4]
        for n in range(ORDER):
            last[group, n] = states[n]
        swap(group).start()

    def combine(s, group):
        if s == 0:
            swap(group).wait_recv()
        else:

            @pl.when(takes(s))
            def _():
                spread(s, 0, group).wait_recv()

            ahead = jnp.maximum(lax.rem(pair, 1 << s) - (1 << (s - 1)), 0)
            ahead = ahead.astype(jnp.float32) * (2.0 * tokens)
        for n in range(ORDER):
            rate = rate_of(n, group)
            if s == 0:
                mine, other = last[group, n], came[0, group, n]
                first = jnp.where(second == 0, mine, other)
                later = jnp.where(second == 0, other, mine)
                window[0, group, n] = later + jnp.exp(-rate * tokens) * first
            else:
                total = jnp.exp(-rate * ahead) * came[s, group, n]
                if s > 1:
                    total = total + carry[group, n]
                if s + 1 < steps:
                    within = jnp.exp(-rate * (2.0 * tokens)) * total
                    window[s, group, n] = window[0, group, n] + within
                    carry[group, n] = total
                else:
                    behind = came[0, group, n] + jnp.exp(-rate * tokens) * total
                    carry[group, n] = jnp.where(second == 0, total, behind)
        if s + 1 < steps:

            @pl.when(sends(s + 1))
            def _():
                for j in range(1 << s):
                    spread(s + 1, j, group).start()

    def finish(group):
        tap = [extra(3 * i, group) for i in range(3)]
        dec = [jnp.exp(-rate_of(n, group)) for n in range(ORDER)]
        first = tuple(coef_of(n, group) * carry[group, n] for n in range(ORDER))

        def step(t, state):
            q2, q1, parts = state
            q0 = rows_at(q_s, t + 2, blocks, group)
            parts = tuple(d * z for d, z in zip(dec, parts))
            long = rounded(rows_at(y_s, t, blocks, group) + tree_sum(parts))
            fq = tap[0] * q0 + tap[1] * q1 + tap[2] * q2
            y_s[pl.ds(pl.multiple_of(t * blocks + group * SUB, SUB), SUB), :] = fq * long
            return (q1, q0, parts)

        start = (rows_at(q_s, 0, blocks, group), rows_at(q_s, 1, blocks, group), first)
        lax.fori_loop(0, tokens, step, start, unroll=4)
        for sub in range(SUB):
            block = group * SUB + sub
            tile = y_s[pl.ds(block, tokens, stride=blocks), :].astype(jnp.bfloat16)
            out[block * LANES : (block + 1) * LANES, :] = flipped(eye, tile).astype(jnp.bfloat16)

    for group in range(groups):
        scan(group)
        for s in range(steps - 1):
            if group > s:
                combine(s, group - 1 - s)
    for late in range(groups, groups + steps - 1):
        for s in range(steps - 1):
            if 0 <= late - 1 - s < groups:
                combine(s, late - 1 - s)
    for group in range(groups):
        combine(steps - 1, group)
        finish(group)

    @pl.when(me + 1 < ctx)
    def _():
        for copy in ends:
            copy.wait_send()

    if inside:
        lax.fori_loop(1, ctx, share_sent, 0)
        lax.fori_loop(0, ctx, all_sent, 0)
    for group in range(groups):
        swap(group).wait_send()
    for s in range(1, steps):

        @pl.when(sends(s))
        def _(s=s):
            for j in range(1 << (s - 1)):
                for group in range(groups):
                    spread(s, j, group).wait_send()


def local_pack(taps, rate_table, residue_table, bias, dp):
    width = bias.shape[0]
    rows = -(-10 // dp)
    extra = jnp.concatenate(
        [taps.reshape(9, width), bias[None], jnp.zeros((rows * dp - 10, width), jnp.float32)]
    )
    own = lax.dynamic_slice_in_dim(extra, lax.axis_index("dp") * rows, rows, 0)
    return jnp.concatenate([rate_table, residue_table, own])


def gathered(packed, dp, ctx):
    height, width = packed.shape
    whole = lax.all_gather(packed, ("dp", "ctx"), axis=0)
    whole = whole.reshape(dp, ctx, height, width).transpose(0, 2, 1, 3)
    return whole.reshape(dp * height, ctx * width // LANES, LANES)


def per_device(dp, ctx, qkv, taps, rate_table, residue_table, bias):
    _, _, chans, tokens = qkv.shape
    blocks = chans // LANES
    modes, width = rate_table.shape
    rows = -(-10 // dp)
    height = 2 * modes + rows
    inside = dp == 4 and width % LANES == 0
    if inside:
        given = (rate_table, residue_table, taps, bias[None])
    else:
        given = (gathered(local_pack(taps, rate_table, residue_table, bias, dp), dp, ctx),)
    groups = blocks // SUB
    steps = (ctx - 1).bit_length()
    wide = (tokens + 2) * blocks
    each = height * max(width // LANES, 1) if inside else 8
    vmem = pl.BlockSpec(memory_space=pltpu.VMEM)
    slab = (groups, ORDER, SUB, LANES)
    f32 = jnp.float32
    out = pl.pallas_call(
        functools.partial(mixer_kernel, dp, ctx, blocks, tokens, inside, rows),
        out_shape=jax.ShapeDtypeStruct((chans, tokens), jnp.bfloat16),
        in_specs=[pl.BlockSpec(memory_space=pl.ANY)] + [vmem] * len(given),
        out_specs=vmem,
        scratch_shapes=[
            pltpu.VMEM((3, chans, tokens), jnp.bfloat16),
            pltpu.VMEM((wide, LANES), f32),
            pltpu.VMEM((wide, LANES), f32),
            pltpu.VMEM((wide, LANES), f32),
            pltpu.VMEM((tokens * blocks, LANES), f32),
            pltpu.VMEM((dp, ctx, each, LANES) if inside else (1, 1, each, LANES), f32),
            pltpu.VMEM((dp * height, blocks, LANES) if inside else (1, SUB, LANES), f32),
            pltpu.VMEM(slab, f32),
            pltpu.VMEM((max(steps - 1, 1),) + slab, f32),
            pltpu.VMEM((steps,) + slab, f32),
            pltpu.VMEM(slab, f32),
            pltpu.SemaphoreType.DMA((groups,)),
            pltpu.SemaphoreType.DMA((ctx,)),
            pltpu.SemaphoreType.DMA((ctx,)),
            pltpu.SemaphoreType.DMA((3, ctx if inside else 1)),
            pltpu.SemaphoreType.DMA((3, ctx if inside else 1)),
            pltpu.SemaphoreType.DMA((3,)),
            pltpu.SemaphoreType.DMA((3,)),
            pltpu.SemaphoreType.DMA((ctx // 2, groups)),
            pltpu.SemaphoreType.DMA((steps, groups)),
        ],
        compiler_params=pltpu.CompilerParams(
            collective_id=0, has_side_effects=True, vmem_limit_bytes=62 * 1024 * 1024
        ),
    )(qkv[0], *given)
    return out[None]


def solution(mesh):
    in_specs = (
        P("dp", None, None, "ctx"),
        P(None, None, "ctx"),
        P("dp", "ctx"),
        P("dp", "ctx"),
        P("ctx"),
    )
    return jax.shard_map(
        functools.partial(per_device, mesh.shape["dp"], mesh.shape["ctx"]),
        mesh=mesh,
        in_specs=in_specs,
        out_specs=P("dp", None, "ctx"),
        check_vma=False,
    )
```

```python
import functools
import jax
import jax.numpy as jnp
from jax import lax
from jax.experimental import pallas as pl
from jax.experimental.pallas import tpu as pltpu
from jax.sharding import PartitionSpec as P

ORDER = 16
LANES = 128
SUB = 8
GROUP = LANES * SUB


def identity(size):
    rows = lax.broadcasted_iota(jnp.int32, (size, size), 0)
    columns = lax.broadcasted_iota(jnp.int32, (size, size), 1)
    return (rows == columns).astype(jnp.bfloat16)


def flipped(eye, block):
    return lax.dot_general(
        eye, block, (((1,), (1,)), ((), ())), preferred_element_type=jnp.float32
    )


def to_tokens(eye, source, target, blocks, group, tokens):
    for sub in range(SUB):
        block = group * SUB + sub
        tile = source[pl.ds(block * LANES, LANES), :]
        target[pl.ds(2 * blocks + block, tokens, stride=blocks), :] = flipped(eye, tile)


def rows_at(ref, token, blocks, group):
    return ref[pl.ds(pl.multiple_of(token * blocks + group * SUB, SUB), SUB), :]


def rounded(value):
    return value.astype(jnp.bfloat16).astype(jnp.float32)


def tree_sum(terms):
    terms = list(terms)
    while len(terms) > 1:
        terms = [a + b for a, b in zip(terms[::2], terms[1::2])]
    return terms[0]


MESH = pl.DeviceIdType.MESH


def mixer_kernel(dp, ctx, blocks, tokens, inside, rows, *refs):
    tables = 4 if inside else 1
    qkv, given = refs[0], refs[1 : 1 + tables]
    refs = refs[tables - 1 :]
    out = refs[2]
    raw, q_s, k_s, v_s, y_s, held, table, last, window, came, carry, load = refs[3:15]
    par_send, par_recv, dp_send, dp_recv, halo_send, halo_recv, step_send, step_recv = refs[15:]
    me = lax.axis_index("ctx")
    own_dp = lax.axis_index("dp")
    groups = blocks // SUB
    steps = (ctx - 1).bit_length()
    pair = lax.div(me, 2)
    second = lax.rem(me, 2)
    modes = ORDER // dp
    height = 2 * modes + rows
    across = lax.rem(own_dp + dp // 2, dp)
    beside = own_dp + 1 - 2 * lax.rem(own_dp, 2)

    def fetch(group):
        own = pl.ds(group * GROUP, GROUP)
        return pltpu.make_async_copy(qkv.at[:, own, :], raw.at[:, own, :], load.at[group])

    for group in range(groups):
        fetch(group).start()

    if inside:
        rate_in, residue_in, taps_in, bias_in = given
        each = blocks // ctx
        for b in range(each):
            lanes = slice(LANES * b, LANES * (b + 1))
            for h in range(modes):
                at = each * h + b
                held[own_dp, me, at : at + 1, :] = rate_in[h : h + 1, lanes]
                at += each * modes
                held[own_dp, me, at : at + 1, :] = residue_in[h : h + 1, lanes]
            for r in range(rows):
                line = bias_in[:, lanes]
                for d in range(dp):
                    e = d * rows + r
                    if e < 9:
                        tap = taps_in[e // 3, e % 3 : e % 3 + 1, lanes]
                        line = jnp.where(own_dp == d, tap, line)
                at = each * (2 * modes + r) + b
                held[own_dp, me, at : at + 1, :] = line

    barrier = pltpu.get_barrier_semaphore()

    def greet(k, _):
        pl.semaphore_signal(
            barrier, inc=1, device_id={"ctx": lax.rem(me + k, ctx)}, device_id_type=MESH
        )
        return 0

    lax.fori_loop(1, ctx, greet, 0)
    greeted = ctx - 1
    if inside:
        for other in (across, beside):
            pl.semaphore_signal(barrier, inc=1, device_id={"dp": other}, device_id_type=MESH)
        greeted += 2
    pl.semaphore_wait(barrier, greeted)

    def remote(source, target, send, recv, where):
        return pltpu.make_async_remote_copy(
            src_ref=source,
            dst_ref=target,
            send_sem=send,
            recv_sem=recv,
            device_id=where,
            device_id_type=MESH,
        )

    def share(k):
        to = {"ctx": lax.rem(me + k, ctx)}
        block = held.at[own_dp, me]
        return remote(block, block, par_send.at[k], par_recv.at[k], to)

    def start_share(k, _):
        share(k).start()
        return 0

    def relay(hop, k):
        from_dp = across if hop == 2 else own_dp
        block = held.at[from_dp, lax.rem(me + ctx - k, ctx)]
        to = across if hop == 0 else beside
        return remote(block, block, dp_send.at[hop, k], dp_recv.at[hop, k], {"dp": to})

    def pass_on(k, _):
        if not isinstance(k, int):
            share(k).wait_recv()
        relay(0, k).start()
        relay(1, k).start()
        return 0

    def pass_far(k, _):
        relay(0, k).wait_recv()
        relay(2, k).start()
        return 0

    def arrive(k, _):
        relay(1, k).wait_recv()
        relay(2, k).wait_recv()
        return 0

    def all_sent(k, _):
        for hop in range(3):
            relay(hop, k).wait_send()
        return 0

    def share_sent(k, _):
        share(k).wait_send()
        return 0

    if inside:
        lax.fori_loop(1, ctx, start_share, 0)
        pass_on(0, 0)

    eye = identity(tokens)

    for group in range(groups):
        fetch(group).wait()
        to_tokens(eye, raw.at[1], k_s, blocks, group, tokens)
        to_tokens(eye, raw.at[2], v_s, blocks, group, tokens)
        if inside and group == groups // 2 - 1:
            lax.fori_loop(1, ctx, pass_on, 0)

    streams = (q_s, k_s, v_s)
    ends = [
        remote(
            ref.at[pl.ds(tokens * blocks, 2 * blocks), :],
            ref.at[pl.ds(0, 2 * blocks), :],
            halo_send.at[w],
            halo_recv.at[w],
            {"ctx": lax.rem(me + 1, ctx)},
        )
        for w, ref in enumerate(streams)
    ]

    @pl.when(me + 1 < ctx)
    def _():
        for copy in ends[1:]:
            copy.start()

    for group in range(groups):
        if inside and group == groups // 2:
            lax.fori_loop(0, ctx, pass_far, 0)
        to_tokens(eye, raw.at[0], q_s, blocks, group, tokens)

    @pl.when(me + 1 < ctx)
    def _():
        ends[0].start()

    @pl.when(me == 0)
    def _():
        for ref in streams:
            ref[0 : 2 * blocks, :] = jnp.zeros((2 * blocks, LANES), jnp.float32)

    def sends(s):
        return lax.rem(pair, 1 << s) == (1 << (s - 1)) - 1

    def takes(s):
        return lax.rem(pair, 1 << s) >= 1 << (s - 1)

    for s in range(1, steps):

        @pl.when(jnp.logical_not(takes(s)))
        def _(s=s):
            came[s] = jnp.zeros_like(came[s])

    if inside:
        lax.fori_loop(0, ctx, arrive, 0)

        def place(d, _):
            for c in range(ctx):
                for h in range(height):
                    table[d * height + h, each * c : each * (c + 1), :] = held[
                        d, c, each * h : each * (h + 1), :
                    ]
            return 0

        lax.fori_loop(0, dp, place, 0)
        source = table
    else:
        source = given[0]

    @pl.when(me > 0)
    def _():
        for copy in ends:
            copy.wait_recv()

    def owned(group):
        return pl.ds(group * SUB, SUB)

    def rate_of(n, group):
        return source[(n // modes) * height + n % modes, owned(group), :]

    def coef_of(n, group):
        residue = source[(n // modes) * height + modes + n % modes, owned(group), :]
        return residue * jnp.sqrt(2.0 * rate_of(n, group) / ORDER)

    def extra(e, group):
        return source[(e // rows) * height + 2 * modes + e % rows, owned(group), :]

    def swap(group):
        return remote(
            last.at[group],
            came.at[0, group],
            step_send.at[0, group],
            step_recv.at[0, group],
            {"ctx": me + 1 - 2 * second},
        )

    def spread(s, j, group):
        return remote(
            window.at[s - 1, group],
            came.at[s, group],
            step_send.at[(1 << (s - 1)) + j, group],
            step_recv.at[s, group],
            {"ctx": lax.rem(me + 2 * (j + 1), ctx)},
        )

    def scan(group):
        tap = [[extra(3 * i + w, group) for i in range(3)] for w in (1, 2)]
        direct = extra(9, group)
        dec = [jnp.exp(-rate_of(n, group)) for n in range(ORDER)]
        coe = [coef_of(n, group) for n in range(ORDER)]

        def step(t, state):
            k2, k1, v2, v1, states = state
            k0 = rows_at(k_s, t + 2, blocks, group)
            v0 = rows_at(v_s, t + 2, blocks, group)
            fk = tap[0][0] * k0 + tap[0][1] * k1 + tap[0][2] * k2
            fv = tap[1][0] * v0 + tap[1][1] * v1 + tap[1][2] * v2
            u = rounded(fk * fv)
            states = tuple(d * s + u for d, s in zip(dec, states))
            y = tree_sum(c * s for c, s in zip(coe, states)) + direct * u
            y_s[pl.ds(pl.multiple_of(t * blocks + group * SUB, SUB), SUB), :] = y
            return (k1, k0, v1, v0, states)

        zero = jnp.zeros((SUB, LANES), jnp.float32)
        start = (
            rows_at(k_s, 0, blocks, group),
            rows_at(k_s, 1, blocks, group),
            rows_at(v_s, 0, blocks, group),
            rows_at(v_s, 1, blocks, group),
            (zero,) * ORDER,
        )
        states = lax.fori_loop(0, tokens, step, start, unroll=4)[4]
        for n in range(ORDER):
            last[group, n] = states[n]
        swap(group).start()

    def combine(s, group):
        if s == 0:
            swap(group).wait_recv()
        else:

            @pl.when(takes(s))
            def _():
                spread(s, 0, group).wait_recv()

            ahead = jnp.maximum(lax.rem(pair, 1 << s) - (1 << (s - 1)), 0)
            ahead = ahead.astype(jnp.float32) * (2.0 * tokens)
        for n in range(ORDER):
            rate = rate_of(n, group)
            if s == 0:
                mine, other = last[group, n], came[0, group, n]
                first = jnp.where(second == 0, mine, other)
                later = jnp.where(second == 0, other, mine)
                window[0, group, n] = later + jnp.exp(-rate * tokens) * first
            else:
                total = jnp.exp(-rate * ahead) * came[s, group, n]
                if s > 1:
                    total = total + carry[group, n]
                if s + 1 < steps:
                    within = jnp.exp(-rate * (2.0 * tokens)) * total
                    window[s, group, n] = window[0, group, n] + within
                    carry[group, n] = total
                else:
                    behind = came[0, group, n] + jnp.exp(-rate * tokens) * total
                    carry[group, n] = jnp.where(second == 0, total, behind)
        if s + 1 < steps:

            @pl.when(sends(s + 1))
            def _():
                for j in range(1 << s):
                    spread(s + 1, j, group).start()

    def finish(group):
        tap = [extra(3 * i, group) for i in range(3)]
        dec = [jnp.exp(-rate_of(n, group)) for n in range(ORDER)]
        first = tuple(coef_of(n, group) * carry[group, n] for n in range(ORDER))

        def step(t, state):
            q2, q1, parts = state
            q0 = rows_at(q_s, t + 2, blocks, group)
            parts = tuple(d * z for d, z in zip(dec, parts))
            long = rounded(rows_at(y_s, t, blocks, group) + tree_sum(parts))
            fq = tap[0] * q0 + tap[1] * q1 + tap[2] * q2
            y_s[pl.ds(pl.multiple_of(t * blocks + group * SUB, SUB), SUB), :] = fq * long
            return (q1, q0, parts)

        start = (rows_at(q_s, 0, blocks, group), rows_at(q_s, 1, blocks, group), first)
        lax.fori_loop(0, tokens, step, start, unroll=4)
        for sub in range(SUB):
            block = group * SUB + sub
            tile = y_s[pl.ds(block, tokens, stride=blocks), :].astype(jnp.bfloat16)
            out[block * LANES : (block + 1) * LANES, :] = flipped(eye, tile).astype(jnp.bfloat16)

    for group in range(groups):
        scan(group)
        for s in range(steps - 1):
            if group > s:
                combine(s, group - 1 - s)
    for late in range(groups, groups + steps - 1):
        for s in range(steps - 1):
            if 0 <= late - 1 - s < groups:
                combine(s, late - 1 - s)
    for group in range(groups):
        combine(steps - 1, group)
        finish(group)

    @pl.when(me + 1 < ctx)
    def _():
        for copy in ends:
            copy.wait_send()

    if inside:
        lax.fori_loop(1, ctx, share_sent, 0)
        lax.fori_loop(0, ctx, all_sent, 0)
    for group in range(groups):
        swap(group).wait_send()
    for s in range(1, steps):

        @pl.when(sends(s))
        def _(s=s):
            for j in range(1 << (s - 1)):
                for group in range(groups):
                    spread(s, j, group).wait_send()


def local_pack(taps, rate_table, residue_table, bias, dp):
    width = bias.shape[0]
    rows = -(-10 // dp)
    extra = jnp.concatenate(
        [taps.reshape(9, width), bias[None], jnp.zeros((rows * dp - 10, width), jnp.float32)]
    )
    own = lax.dynamic_slice_in_dim(extra, lax.axis_index("dp") * rows, rows, 0)
    return jnp.concatenate([rate_table, residue_table, own])


def gathered(packed, dp, ctx):
    height, width = packed.shape
    whole = lax.all_gather(packed, ("dp", "ctx"), axis=0)
    whole = whole.reshape(dp, ctx, height, width).transpose(0, 2, 1, 3)
    return whole.reshape(dp * height, ctx * width // LANES, LANES)


def per_device(dp, ctx, qkv, taps, rate_table, residue_table, bias):
    _, _, chans, tokens = qkv.shape
    blocks = chans // LANES
    modes, width = rate_table.shape
    rows = -(-10 // dp)
    height = 2 * modes + rows
    inside = dp == 4 and width % LANES == 0
    if inside:
        given = (rate_table, residue_table, taps, bias[None])
    else:
        given = (gathered(local_pack(taps, rate_table, residue_table, bias, dp), dp, ctx),)
    groups = blocks // SUB
    steps = (ctx - 1).bit_length()
    wide = (tokens + 2) * blocks
    each = height * max(width // LANES, 1) if inside else 8
    vmem = pl.BlockSpec(memory_space=pltpu.VMEM)
    slab = (groups, ORDER, SUB, LANES)
    f32 = jnp.float32
    out = pl.pallas_call(
        functools.partial(mixer_kernel, dp, ctx, blocks, tokens, inside, rows),
        out_shape=jax.ShapeDtypeStruct((chans, tokens), jnp.bfloat16),
        in_specs=[pl.BlockSpec(memory_space=pl.ANY)] + [vmem] * len(given),
        out_specs=vmem,
        scratch_shapes=[
            pltpu.VMEM((3, chans, tokens), jnp.bfloat16),
            pltpu.VMEM((wide, LANES), f32),
            pltpu.VMEM((wide, LANES), f32),
            pltpu.VMEM((wide, LANES), f32),
            pltpu.VMEM((tokens * blocks, LANES), f32),
            pltpu.VMEM((dp, ctx, each, LANES) if inside else (1, 1, each, LANES), f32),
            pltpu.VMEM((dp * height, blocks, LANES) if inside else (1, SUB, LANES), f32),
            pltpu.VMEM(slab, f32),
            pltpu.VMEM((max(steps - 1, 1),) + slab, f32),
            pltpu.VMEM((steps,) + slab, f32),
            pltpu.VMEM(slab, f32),
            pltpu.SemaphoreType.DMA((groups,)),
            pltpu.SemaphoreType.DMA((ctx,)),
            pltpu.SemaphoreType.DMA((ctx,)),
            pltpu.SemaphoreType.DMA((3, ctx if inside else 1)),
            pltpu.SemaphoreType.DMA((3, ctx if inside else 1)),
            pltpu.SemaphoreType.DMA((3,)),
            pltpu.SemaphoreType.DMA((3,)),
            pltpu.SemaphoreType.DMA((ctx // 2, groups)),
            pltpu.SemaphoreType.DMA((steps, groups)),
        ],
        compiler_params=pltpu.CompilerParams(
            collective_id=0, has_side_effects=True, vmem_limit_bytes=61 * 1024 * 1024
        ),
    )(qkv[0], *given)
    return out[None]


def solution(mesh):
    in_specs = (
        P("dp", None, None, "ctx"),
        P(None, None, "ctx"),
        P("dp", "ctx"),
        P("dp", "ctx"),
        P("ctx"),
    )
    return jax.shard_map(
        functools.partial(per_device, mesh.shape["dp"], mesh.shape["ctx"]),
        mesh=mesh,
        in_specs=in_specs,
        out_specs=P("dp", None, "ctx"),
        check_vma=False,
    )
```
